32 devices in a mesh: groups: 2 (over x), row: 4 (over z), col: 4 (over y, core).
Axes of the slice: x: 2, y: 2, z: 4, core: 2. Of those that a mesh axis runs over, the one named last changes fastest.
Arguments:
- src_feats: bfloat16 [32768, 256], P(('groups', 'row', 'col')), parts along dimension 0, may hold values from -6 to 6
- dst_feats: bfloat16 [32768, 256], P(('groups', 'col', 'row')), parts along dimension 0, may hold values from -6 to 6
- w_self: bfloat16 [256, 256], replicated, may hold values from -0.375 to 0.375
- w_neigh: bfloat16 [256, 256], replicated, may hold values from -0.375 to 0.375
- bias: float32 [256], replicated, may hold values from -2.5 to 2.5
- cotangent: bfloat16 [32768, 256], P(('groups', 'col', 'row')), parts along dimension 0, may hold values from -6 to 6
- tile_vals: bfloat16 [8, 4, 32, 128, 128], P(('groups', 'col'), 'row'), parts along dimension 0
- tile_rows: int32 [8, 4, 32], P(('groups', 'col'), 'row'), parts along dimension 0, may hold values from 0 to 31
- tile_cols: int32 [8, 4, 32], P(('groups', 'col'), 'row'), parts along dimension 0, may hold values from 0 to 31
- tile_count: int32 [8, 4], P(('groups', 'col'), 'row'), parts along dimension 0, may hold values from 6 to 32, as said below
Outputs:
- hidden_out: bfloat16 [32768, 256], P(('groups', 'col', 'row')), parts along dimension 0
- grad_src: bfloat16 [32768, 256], P(('groups', 'row', 'col')), parts along dimension 0
- grad_dst: bfloat16 [32768, 256], P(('groups', 'col', 'row')), parts along dimension 0
- grad_w_self: float32 [512, 256], P('groups'), parts along dimension 0
- grad_w_neigh: float32 [512, 256], P('groups'), parts along dimension 0
- grad_bias: float32 [512], P('groups'), parts along dimension 0
The draws below stay inside these ranges and needn't reach their ends.
There are 2 independent parts, one for each index of `groups`. The reference program is written for one: setup_inputs(seed, part) draws one part's arguments, and reference() takes and returns one part's arrays. A program takes and returns all parts, laid end to end along the dimension named above; an argument that names none is the same for every part. Nothing has to cross between parts.
Inputs may be any that keep to these rules, and one draw needn't show every extreme that they name: `tile_count`: live slots of a cell, those before its count, name distinct tile positions; the largest count is exactly 32 in every draw.
All inputs are finite; a program needn't handle non-finite values.
Results may differ from the reference program's by a relative error of at most 0.009.
Values may be sent and summed in bfloat16 or wider, within the bound.
A program may use at most 128 MiB of HBM per device.

```python
import math
import jax
import jax.numpy as jnp
from jax import lax

F = 256
TILE = 128
NODES = 16384
ROWS_C = 4096
COLS_R = 4096
RB = 32
CB = 32
TCAP = 32
N_ROW = 4
N_COL = 4


def tile_pattern(key):
    cells = N_COL * N_ROW
    lowest = max(1, TCAP // 5)
    highest = max(lowest, TCAP * 3 // 5)
    counts = jax.random.randint(jax.random.fold_in(key, 101), (cells,), lowest, highest + 1)
    chosen = jax.random.randint(jax.random.fold_in(key, 102), (), 0, cells)
    counts = jnp.where(jnp.arange(cells) == chosen, TCAP, counts).astype(jnp.int32)
    cell_keys = jax.random.split(jax.random.fold_in(key, 103), cells)

    def pick_slots(cell_key):
        return jax.random.permutation(cell_key, RB * CB)[:TCAP]
    slots = jax.vmap(pick_slots)(cell_keys).astype(jnp.int32)
    slot_rows = (slots // CB).reshape(N_COL, N_ROW, TCAP)
    slot_cols = (slots % CB).reshape(N_COL, N_ROW, TCAP)
    return (counts.reshape(N_COL, N_ROW), slot_rows, slot_cols)


def draw_tile_count(key, part):
    counts, slot_rows, slot_cols = tile_pattern(key)
    return counts


def draw_tile_rows(key, part):
    counts, slot_rows, slot_cols = tile_pattern(key)
    return slot_rows


def draw_tile_cols(key, part):
    counts, slot_rows, slot_cols = tile_pattern(key)
    return slot_cols


def draw_tile_vals(key, part):
    key = jax.random.fold_in(key, 7)
    shape = (N_COL, N_ROW, TCAP, TILE, TILE)
    present = jax.random.bernoulli(jax.random.fold_in(key, 1), 0.5, shape).astype(jnp.float32)
    level = jax.random.uniform(jax.random.fold_in(key, 2), shape, jnp.float32, 0.5, 1.5)
    per_block = max(1.0, N_ROW * 0.4 * TCAP / RB)
    scaling = 1.0 / math.sqrt(0.54 * TILE * per_block)
    return (present * level * scaling).astype(jnp.bfloat16)


def block_levels(stream_key, extent, shards, low, high):
    gain = 1.0
    for axis_at, shards_of in shards:
        draws = jax.random.uniform(jax.random.fold_in(jax.random.fold_in(stream_key, 6), axis_at), (shards_of,), jnp.float32, low / len(shards), high / len(shards))
        gain = gain * jnp.repeat(jnp.exp(draws), extent[axis_at] // shards_of).reshape((-1,) + (1,) * (len(extent) - 1 - axis_at))
    return gain


def gaussian(key, extent, width, reach, shards=(), kind=jnp.bfloat16):
    loudness = block_levels(key, extent, shards, -0.22, 0.18) if shards else 1.0
    array = jax.random.normal(key, extent, jnp.float32) * width * loudness
    return jnp.minimum(jnp.maximum(array, -reach), reach).astype(kind)


def setup_inputs(seed: int = 0, part: int = 0) -> dict:
    arg_keys = jax.random.split(jax.random.key(seed), 11)
    part_keys = jax.random.split(jax.random.fold_in(arg_keys[10], part), 11)
    return {
        "src_feats": gaussian(part_keys[0], (NODES, F), 1.0, 6.0, ((0, 16),)),
        "dst_feats": gaussian(part_keys[1], (NODES, F), 1.0, 6.0, ((0, 16),)),
        "w_self": gaussian(arg_keys[2], (F, F), F ** -0.5, 0.375),
        "w_neigh": gaussian(arg_keys[3], (F, F), F ** -0.5, 0.375),
        "bias": gaussian(arg_keys[4], (F,), 0.5, 2.5, (), jnp.float32),
        "cotangent": gaussian(part_keys[5], (NODES, F), 1.0, 6.0, ((0, 16),)),
        "tile_vals": draw_tile_vals(jax.random.fold_in(jax.random.fold_in(arg_keys[10], part), 71), part),
        "tile_rows": draw_tile_rows(jax.random.fold_in(jax.random.fold_in(arg_keys[10], part), 71), part),
        "tile_cols": draw_tile_cols(jax.random.fold_in(jax.random.fold_in(arg_keys[10], part), 71), part),
        "tile_count": draw_tile_count(jax.random.fold_in(jax.random.fold_in(arg_keys[10], part), 71), part),
    }


def silu_parts(preact):
    gate_sig = jax.nn.sigmoid(preact)
    return (preact * gate_sig, gate_sig * (1.0 + preact * (1.0 - gate_sig)))

def round_partials(partials):
    rounded = lax.optimization_barrier(partials.astype(jnp.bfloat16))
    return lax.optimization_barrier(jnp.sum(rounded.astype(jnp.float32), axis=0))

def reference(src_feats, dst_feats, w_self, w_neigh, bias, cotangent, tile_vals, tile_rows, tile_cols, tile_count):
    live_mask = jnp.arange(TCAP, dtype=jnp.int32)[None, None, :] < tile_count[:, :, None]
    src_blocks = src_feats.reshape(N_ROW, CB, TILE, F)

    def forward_cell(cell):
        cell_vals, cell_rows, cell_cols, cell_live = cell

        def one_cell(blocks, vals_here, rows_here, cols_here, live_here):
            kept = jnp.where(live_here[:, None, None], vals_here, jnp.zeros((), vals_here.dtype))
            picked = blocks[cols_here].astype(jnp.float32)
            product = jnp.einsum('tij,tjf->tif', kept.astype(jnp.float32), picked)
            return jnp.zeros((RB, TILE, F), jnp.float32).at[rows_here].add(product)
        partials = jax.vmap(one_cell)(src_blocks, cell_vals, cell_rows, cell_cols, cell_live)
        return round_partials(partials).reshape(ROWS_C, F).astype(jnp.bfloat16)
    aggregate = lax.map(forward_cell, (tile_vals, tile_rows, tile_cols, live_mask)).reshape(NODES, F)
    preact = jnp.dot(dst_feats, w_self, preferred_element_type=jnp.float32)
    preact = preact + jnp.dot(aggregate, w_neigh, preferred_element_type=jnp.float32) + bias
    hidden_f, slope = silu_parts(preact)
    hidden_out = hidden_f.astype(jnp.bfloat16)
    grad_pre = (cotangent.astype(jnp.float32) * slope).astype(jnp.bfloat16)
    back_feats = jnp.dot(grad_pre, w_neigh.T, preferred_element_type=jnp.float32).astype(jnp.bfloat16)
    grad_dst = jnp.dot(grad_pre, w_self.T, preferred_element_type=jnp.float32).astype(jnp.bfloat16)
    back_blocks = back_feats.reshape(N_COL, RB, TILE, F)

    def backward_cell(column_index):
        cell_vals = tile_vals[:, column_index]
        cell_rows = tile_rows[:, column_index]
        cell_cols = tile_cols[:, column_index]
        cell_live = live_mask[:, column_index]

        def one_cell(blocks, vals_here, rows_here, cols_here, live_here):
            kept = jnp.where(live_here[:, None, None], vals_here, jnp.zeros((), vals_here.dtype))
            picked = blocks[rows_here].astype(jnp.float32)
            product = jnp.einsum('tji,tjf->tif', kept.astype(jnp.float32), picked)
            return jnp.zeros((CB, TILE, F), jnp.float32).at[cols_here].add(product)
        partials = jax.vmap(one_cell)(back_blocks, cell_vals, cell_rows, cell_cols, cell_live)
        return round_partials(partials).reshape(COLS_R, F).astype(jnp.bfloat16)
    grad_src = lax.map(backward_cell, jnp.arange(N_ROW, dtype=jnp.int32)).reshape(NODES, F)
    scaling = 1.0 / math.sqrt(NODES)
    grad_w_self = jnp.dot(dst_feats.T, grad_pre, preferred_element_type=jnp.float32) * scaling
    grad_w_neigh = jnp.dot(aggregate.T, grad_pre, preferred_element_type=jnp.float32) * scaling
    grad_bias = lax.optimization_barrier(jnp.sum(grad_pre.astype(jnp.float32), axis=0)) * scaling
    return (hidden_out, grad_src, grad_dst, grad_w_self, grad_w_neigh, grad_bias)
```

```python
import functools
import math

import jax
import jax.numpy as jnp
from jax import lax
from jax.experimental import pallas as pl
from jax.experimental.pallas import tpu as pltpu
from jax.sharding import PartitionSpec as P

MESH = pl.DeviceIdType.MESH
CHUNKS = 4


def accumulate(tile_vals, out_index, in_index, live_count, source, out_blocks, flipped):
    tile_size = tile_vals.shape[-1]
    feature_width = source.shape[1]
    slot_total = tile_vals.shape[0]
    blocks = source.reshape(-1, tile_size, feature_width)
    group_size = min(32, slot_total)
    einsum_form = "tji,tjf->tif" if flipped else "tij,tjf->tif"

    def add_group(group_number, totals):
        first = group_number * group_size
        part_vals = lax.dynamic_slice_in_dim(tile_vals, first, group_size, 0)
        part_in = lax.dynamic_slice_in_dim(in_index, first, group_size, 0)
        part_out = lax.dynamic_slice_in_dim(out_index, first, group_size, 0)
        live = first + jnp.arange(group_size, dtype=jnp.int32) < live_count
        part_vals = jnp.where(live[:, None, None], part_vals, jnp.zeros((), part_vals.dtype))
        gathered = jnp.take(blocks, part_in, axis=0)
        product = jnp.einsum(einsum_form, part_vals, gathered, preferred_element_type=jnp.float32)
        return totals.at[part_out].add(product)

    initial = jnp.zeros((out_blocks, tile_size, feature_width), jnp.float32)
    turn_count = slot_total // group_size
    totals = lax.fori_loop(0, turn_count, add_group, initial)
    return totals.reshape(out_blocks * tile_size, feature_width)


def rounded_term(values):
    narrow = lax.optimization_barrier(values.astype(jnp.bfloat16))
    return narrow.astype(jnp.float32)


def dense_step(dst_rows, agg_rows, cot_rows, w_self, w_neigh, bias):
    preact = jnp.dot(dst_rows, w_self, preferred_element_type=jnp.float32)
    preact = preact + jnp.dot(agg_rows, w_neigh, preferred_element_type=jnp.float32) + bias
    gate_sig = jax.nn.sigmoid(preact)
    hidden_rows = (preact * gate_sig).astype(jnp.bfloat16)
    slope = gate_sig * (1.0 + preact * (1.0 - gate_sig))
    grad_rows = (cot_rows.astype(jnp.float32) * slope).astype(jnp.bfloat16)
    return (hidden_rows, grad_rows)


def local(
    src_feats,
    dst_feats,
    w_self,
    w_neigh,
    bias,
    cotangent,
    tile_vals,
    tile_rows,
    tile_cols,
    tile_count,
):
    cell_vals = tile_vals[0, 0]
    cell_rows = tile_rows[0, 0]
    cell_cols = tile_cols[0, 0]
    live_count = tile_count[0, 0]
    tile_size = cell_vals.shape[-1]
    own_rows = dst_feats.shape[0]
    row_blocks = own_rows * lax.axis_size("row") // tile_size
    col_blocks = src_feats.shape[0] * lax.axis_size("col") // tile_size
    source_block = lax.all_gather(src_feats, "col", axis=0, tiled=True)
    partial_value = rounded_term(
        accumulate(cell_vals, cell_rows, cell_cols, live_count, source_block, row_blocks, False)
    )
    aggregate = lax.psum_scatter(
        partial_value.astype(jnp.bfloat16), "row", scatter_dimension=0, tiled=True
    )
    hidden_out, grad_pre = dense_step(dst_feats, aggregate, cotangent, w_self, w_neigh, bias)
    back_own = jnp.dot(grad_pre, w_neigh.T, preferred_element_type=jnp.float32).astype(jnp.bfloat16)
    back_feats = lax.all_gather(back_own, "row", axis=0, tiled=True)
    grad_dst = jnp.dot(grad_pre, w_self.T, preferred_element_type=jnp.float32).astype(jnp.bfloat16)
    back_partial = rounded_term(
        accumulate(cell_vals, cell_cols, cell_rows, live_count, back_feats, col_blocks, True)
    )
    grad_src = lax.psum_scatter(
        back_partial.astype(jnp.bfloat16), "col", scatter_dimension=0, tiled=True
    )
    term_self = jnp.dot(dst_feats.T, grad_pre, preferred_element_type=jnp.float32)
    term_neigh = jnp.dot(aggregate.T, grad_pre, preferred_element_type=jnp.float32)
    term_bias = jnp.sum(grad_pre.astype(jnp.float32), axis=0)
    sum_self, sum_neigh, sum_bias = lax.psum((term_self, term_neigh, term_bias), ("row", "col"))
    scaling = 1.0 / math.sqrt(own_rows * lax.axis_size("row") * lax.axis_size("col"))
    return (
        hidden_out,
        grad_src,
        grad_dst,
        sum_self * scaling,
        sum_neigh * scaling,
        sum_bias * scaling,
    )


def sage_kernel(
    sizes, scaling, idx, src, dst_hbm, w_self, w_neigh, bias, cot_hbm, vals_hbm,
    hidden, grad_src, grad_dst, grads,
    dst, cot, vals, gathered, sums, part, from_low, from_high, back, grads_in,
    back_part, pair_in, chip_in, term_acc, terms, terms_in, terms_row,
    load_sem, src_send, src_recv, fwd_send, red_send, up_recv, down_recv,
    own_send, pass_send, back_recv, pair_send, pair_recv, chip_send, chip_recv,
    t1_send, t1_recv, t2_send, t2_recv, t3_send, t3_recv,
):
    rows_n, cols_n, slots, blocks, chunks, piece = sizes
    chips_n = cols_n // 2
    per = blocks // chunks
    tile = src.shape[1]
    width = src.shape[2]
    row_blocks = rows_n * blocks
    col_blocks = cols_n * blocks
    z = lax.axis_index("row")
    c = lax.axis_index("col")
    chip = c // 2
    core = c % 2
    sibling = chip * 2 + (1 - core)
    f32, bf16 = jnp.float32, jnp.bfloat16

    def remote(src_ref, dst_ref, send, recv, device):
        return pltpu.make_async_remote_copy(
            src_ref=src_ref, dst_ref=dst_ref, send_sem=send, recv_sem=recv,
            device_id=device, device_id_type=MESH,
        )

    loads = [
        pltpu.make_async_copy(src, gathered.at[pl.ds(c * blocks, blocks)], load_sem.at[0]),
        pltpu.make_async_copy(vals_hbm, vals, load_sem.at[1]),
        pltpu.make_async_copy(dst_hbm, dst, load_sem.at[2]),
        pltpu.make_async_copy(cot_hbm, cot, load_sem.at[3]),
    ]
    for load in loads:
        load.start()

    barrier = pltpu.get_barrier_semaphore()
    for k in range(1, cols_n):
        pl.semaphore_signal(barrier, inc=1, device_id={"col": lax.rem(c + k, cols_n)}, device_id_type=MESH)
    for k in range(1, rows_n):
        pl.semaphore_signal(barrier, inc=1, device_id={"row": lax.rem(z + k, rows_n)}, device_id_type=MESH)
    pl.semaphore_wait(barrier, cols_n + rows_n - 2)

    def src_copy(owner, k, sem_at, device, first):
        at = pl.ds(owner * blocks + k * per, per)
        from_ref = src.at[pl.ds(k * per, per)] if first else gathered.at[at]
        return remote(from_ref, gathered.at[at], src_send.at[sem_at, k], src_recv.at[owner, k], {"col": device})

    def far(dy):
        return lax.rem(chip + dy, chips_n) * 2 + core

    for k in range(chunks):
        for dy in range(1, chips_n):
            src_copy(c, k, dy, far(dy), True).start()
    for k in range(chunks):
        src_copy(c, k, 0, sibling, True).start()

    def src_pass(dy, k):
        owner = far(dy)
        at = pl.ds(owner * blocks + k * per, per)
        return remote(gathered.at[at], gathered.at[at], fwd_send.at[dy, k], src_recv.at[owner, k], {"col": sibling})

    sums[slots] = jnp.zeros((tile, width), f32)
    term_acc[...] = jnp.zeros_like(term_acc)

    for k in range(chunks):
        for dy in range(1, chips_n):
            src_copy(far(dy), k, dy, sibling, False).wait_recv()
            src_pass(dy, k).start()
    for load in loads[:2]:
        load.wait()
    for k in range(chunks):
        for y in range(chips_n):
            src_copy(y * 2 + 1 - core, k, 0, sibling, False).wait_recv()

    def forward_slot(s, carry):
        product = jnp.dot(vals[s], gathered[idx[1, s]], preferred_element_type=f32)
        sums[s] = product + sums[idx[2, s]]
        return carry

    lax.fori_loop(0, slots, forward_slot, 0)

    def forward_row(i, carry):
        part[i] = sums[idx[4, i]].astype(bf16)
        return carry

    lax.fori_loop(0, row_blocks, forward_row, 0)

    def at_of(d, k):
        return pl.ds(d * blocks + k * per, per)

    def up_copy(d, k, device):
        return remote(part.at[at_of(d, k)], from_low.at[at_of(d, k)], red_send.at[d, k], up_recv.at[d, k], {"row": device})

    def down_copy(d, k, device):
        return remote(part.at[at_of(d, k)], from_high.at[at_of(d, k)], red_send.at[d, k], down_recv.at[d, k], {"row": device})

    next_up = lax.rem(z + 1, rows_n)
    next_down = lax.rem(z + rows_n - 1, rows_n)

    def add_in(d, k, buf):
        at = at_of(d, k)
        part[at] = (part[at].astype(f32) + buf[at].astype(f32)).astype(bf16)

    def send_up(k):
        def step(i, carry):
            d = rows_n - 1 - i

            @pl.when(z > 0)
            def _():
                up_copy(d, k, next_up).wait_recv()
                add_in(d, k, from_low)

            up_copy(d, k, next_up).start()
            return carry

        lax.fori_loop(0, rows_n - 1 - z, step, 0)

    def send_down(k):
        def step(d, carry):
            @pl.when(z < rows_n - 1)
            def _():
                down_copy(d, k, next_down).wait_recv()
                add_in(d, k, from_high)

            down_copy(d, k, next_down).start()
            return carry

        lax.fori_loop(0, z, step, 0)

    is_end = jnp.logical_or(z == 0, z == rows_n - 1)
    is_low = z < rows_n // 2

    def stage_a(k):
        @pl.when(is_low)
        def _():
            send_up(k)

        @pl.when(jnp.logical_not(is_low))
        def _():
            send_down(k)

    def stage_b(k):
        @pl.when(is_low)
        def _():
            send_down(k)

        @pl.when(jnp.logical_not(is_low))
        def _():
            send_up(k)

    @pl.when(is_end)
    def _():
        def each(k, carry):
            stage_a(k)
            return carry

        lax.fori_loop(0, chunks, each, 0)

    for load in loads[2:]:
        load.wait()

    def own_copy(k, way, device):
        at = at_of(z, k)
        return remote(back.at[at], back.at[at], own_send.at[way, k], back_recv.at[z, k], {"row": device})

    def pass_copy(owner, k, device):
        at = at_of(owner, k)
        return remote(back.at[at], back.at[at], pass_send.at[owner, k], back_recv.at[owner, k], {"row": device})

    def finish(k):
        @pl.when(z > 0)
        def _():
            up_copy(z, k, next_up).wait_recv()
            add_in(z, k, from_low)

        @pl.when(z < rows_n - 1)
        def _():
            down_copy(z, k, next_down).wait_recv()
            add_in(z, k, from_high)

        at = pl.ds(k * per, per)
        flat = (per * tile, width)
        agg_rows = part[at_of(z, k)].reshape(flat)
        dst_rows = dst[at].reshape(flat)
        preact = jnp.dot(dst_rows, w_self[...], preferred_element_type=f32)
        preact = preact + jnp.dot(agg_rows, w_neigh[...], preferred_element_type=f32) + bias[...]
        gate_sig = jax.nn.sigmoid(preact)
        slope = gate_sig * (1.0 + preact * (1.0 - gate_sig))
        grad_rows = (cot[at].reshape(flat).astype(f32) * slope).astype(bf16)
        turned = (((1,), (1,)), ((), ()))
        back_rows = lax.dot_general(grad_rows, w_neigh[...], turned, preferred_element_type=f32)
        back[at_of(z, k)] = back_rows.astype(bf16).reshape((per, tile, width))

        @pl.when(z < rows_n - 1)
        def _():
            own_copy(k, 0, next_up).start()

        @pl.when(z > 0)
        def _():
            own_copy(k, 1, next_down).start()

        hidden[at] = (preact * gate_sig).astype(bf16).reshape((per, tile, width))
        dst_grad = lax.dot_general(grad_rows, w_self[...], turned, preferred_element_type=f32)
        grad_dst[at] = dst_grad.astype(bf16).reshape((per, tile, width))
        outer = (((0,), (0,)), ((), ()))
        term_acc[pl.ds(0, width)] += lax.dot_general(dst_rows, grad_rows, outer, preferred_element_type=f32)
        term_acc[pl.ds(width, width)] += lax.dot_general(agg_rows, grad_rows, outer, preferred_element_type=f32)
        term_acc[pl.ds(2 * width, 8)] += jnp.sum(grad_rows.astype(f32).reshape((per * tile // 8, 8, width)), axis=0)

    def pass_on(j, k):
        @pl.when(jnp.logical_and(z >= j, z < rows_n - 1))
        def _():
            copy = pass_copy(z - j, k, next_up)
            copy.wait_recv()
            copy.start()

        @pl.when(jnp.logical_and(z + j < rows_n, z > 0))
        def _():
            copy = pass_copy(z + j, k, next_down)
            copy.wait_recv()
            copy.start()

    def turn(t, carry):
        @pl.when(jnp.logical_and(t < chunks, jnp.logical_not(is_end)))
        def _():
            stage_a(t)

        @pl.when(jnp.logical_and(t >= 1, t <= chunks))
        def _():
            stage_b(t - 1)
            finish(t - 1)

        for j in range(1, rows_n - 1):
            @pl.when(jnp.logical_and(t >= 1 + j, t <= chunks + j))
            def _():
                pass_on(j, t - 1 - j)

        return carry

    lax.fori_loop(0, chunks + 1, turn, 0)

    bias_sum = jnp.sum(term_acc[pl.ds(2 * width, 8)], axis=0, keepdims=True)
    spot = lax.broadcasted_iota(jnp.int32, (16, width), 0) == 0
    terms[pl.ds(0, 2 * width)] = term_acc[...][: 2 * width].astype(bf16)
    terms[pl.ds(2 * width, 16)] = jnp.where(spot, bias_sum, 0.0).astype(bf16)
    if cols_n * piece > 2 * width + 16:
        rest = cols_n * piece - 2 * width - 16
        terms[pl.ds(2 * width + 16, rest)] = jnp.zeros((rest, width), bf16)

    def t1_copy(k):
        peer = lax.rem(c + k, cols_n)
        return remote(terms.at[pl.ds(peer * piece, piece)], terms_in.at[k - 1], t1_send.at[k - 1], t1_recv.at[k - 1], {"col": peer})

    def t2_copy(k):
        peer = lax.rem(z + k, rows_n)
        return remote(terms_row.at[z], terms_row.at[z], t2_send.at[k - 1], t2_recv.at[k - 1], {"row": peer})

    def t3_copy(k):
        peer = lax.rem(c + k, cols_n)
        at = pl.ds(c * piece, piece)
        return remote(grads_in.at[at], grads_in.at[at], t3_send.at[k - 1], t3_recv.at[k - 1], {"col": peer})

    for k in range(1, cols_n):
        t1_copy(k).start()

    lax.fori_loop(chunks + 1, chunks + rows_n - 1, turn, 0)

    total = terms[pl.ds(c * piece, piece)].astype(f32)
    for k in range(1, cols_n):
        t1_copy(k).wait_recv()
        total = total + terms_in[k - 1].astype(f32)
    terms_row[z] = total.astype(bf16)
    for k in range(1, rows_n):
        t2_copy(k).start()

    @pl.when(z == rows_n - 1)
    def _():
        for owner in range(rows_n - 1):
            for k in range(chunks):
                pass_copy(owner, k, next_down).wait_recv()

    @pl.when(z == 0)
    def _():
        for owner in range(1, rows_n):
            for k in range(chunks):
                pass_copy(owner, k, next_up).wait_recv()

    for k in range(1, rows_n):
        t2_copy(k).wait_recv()
    whole = terms_row[0].astype(f32)
    for k in range(1, rows_n):
        whole = whole + terms_row[k].astype(f32)
    grads_in[pl.ds(c * piece, piece)] = whole * scaling
    for k in range(1, cols_n):
        t3_copy(k).start()

    def backward_slot(s, carry):
        product = lax.dot_general(vals[s], back[idx[0, s]], (((0,), (0,)), ((), ())), preferred_element_type=f32)
        sums[s] = product + sums[idx[3, s]]
        return carry

    lax.fori_loop(0, slots, backward_slot, 0)

    def backward_block(owner):
        def each(i, carry):
            at = owner * blocks + i
            back_part[at] = sums[idx[5, at]].astype(bf16)
            return carry

        lax.fori_loop(0, blocks, each, 0)

    def pair_copy(dy, k):
        y = lax.rem(chip + dy, chips_n)
        owner = y * 2 + 1 - core
        return remote(
            back_part.at[at_of(owner, k)], pair_in.at[at_of(dy, k)],
            pair_send.at[dy, k], pair_recv.at[dy, k], {"col": sibling},
        )

    def chip_copy(dy, k):
        return remote(
            back_part.at[at_of(far(dy), k)], chip_in.at[at_of(dy, k)],
            chip_send.at[dy, k], chip_recv.at[dy, k], {"col": far(dy)},
        )

    order = list(range(1, chips_n)) + [0]
    for dy in order:
        backward_block(lax.rem(chip + dy, chips_n) * 2 + 1 - core)
        for k in range(chunks):
            pair_copy(dy, k).start()
        backward_block(far(dy))
    for dy in order:
        for k in range(chunks):
            pair_copy(dy, k).wait_recv()
            at = at_of(far(dy), k)
            back_part[at] = (back_part[at].astype(f32) + pair_in[at_of(dy, k)].astype(f32)).astype(bf16)
            if dy:
                chip_copy(dy, k).start()
    for k in range(chunks):
        summed = back_part[at_of(c, k)].astype(f32)
        for dy in range(1, chips_n):
            chip_copy(dy, k).wait_recv()
            summed = summed + chip_in[at_of(dy, k)].astype(f32)
        grad_src[pl.ds(k * per, per)] = summed.astype(bf16)

    for k in range(1, cols_n):
        t3_copy(k).wait_recv()
    grads[...] = grads_in[...]

    for k in range(chunks):
        src_copy(c, k, 0, sibling, True).wait_send()
        for dy in range(1, chips_n):
            src_copy(c, k, dy, far(dy), True).wait_send()
            src_pass(dy, k).wait_send()
            chip_copy(dy, k).wait_send()
        for dy in range(chips_n):
            pair_copy(dy, k).wait_send()
        for d in range(rows_n):
            @pl.when(z != d)
            def _():
                up_copy(d, k, next_up).wait_send()

        @pl.when(z < rows_n - 1)
        def _():
            own_copy(k, 0, next_up).wait_send()

        @pl.when(z > 0)
        def _():
            own_copy(k, 1, next_down).wait_send()

        for d in range(rows_n):
            @pl.when(jnp.logical_and(z != d, jnp.logical_not(is_end)))
            def _():
                pass_copy(d, k, next_up).wait_send()
    for k in range(1, cols_n):
        t1_copy(k).wait_send()
        t3_copy(k).wait_send()
    for k in range(1, rows_n):
        t2_copy(k).wait_send()


def slot_links(keys, live, blocks):
    slots = keys.shape[0]
    place = jnp.arange(slots, dtype=jnp.int32)
    same = (keys[:, None] == keys[None, :]) & live[None, :] & (place[None, :] < place[:, None])
    before = jnp.max(jnp.where(same, place[None, :], -1), axis=1)
    hit = (jnp.arange(blocks, dtype=jnp.int32)[:, None] == keys[None, :]) & live[None, :]
    last = jnp.max(jnp.where(hit, place[None, :], -1), axis=1)
    return jnp.where(before < 0, slots, before), jnp.where(last < 0, slots, last)


def fused(src_feats, dst_feats, w_self, w_neigh, bias, cotangent, tile_vals, tile_rows, tile_cols, tile_count):
    cell_vals, cell_rows, cell_cols = tile_vals[0, 0], tile_rows[0, 0], tile_cols[0, 0]
    slots, tile = cell_vals.shape[:2]
    own_rows, width = src_feats.shape
    rows_n, cols_n = lax.axis_size("row"), lax.axis_size("col")
    blocks = own_rows // tile
    chunks = CHUNKS
    row_blocks, col_blocks = rows_n * blocks, cols_n * blocks
    piece = -(-(2 * width + 16) // (16 * cols_n)) * 16
    live = jnp.arange(slots, dtype=jnp.int32) < tile_count[0, 0]
    row_prev, row_last = slot_links(cell_rows, live, row_blocks)
    col_prev, col_last = slot_links(cell_cols, live, col_blocks)
    most = max(slots, row_blocks, col_blocks)
    lists = (cell_rows, cell_cols, row_prev, col_prev, row_last, col_last)
    idx = jnp.stack([jnp.pad(v, (0, most - v.shape[0])) for v in lists])
    scaling = 1.0 / math.sqrt(own_rows * rows_n * cols_n)
    sizes = (rows_n, cols_n, slots, blocks, chunks, piece)
    bf16, f32 = jnp.bfloat16, jnp.float32
    cube = lambda n: pltpu.VMEM((n, tile, width), bf16)
    dma = lambda *shape: pltpu.SemaphoreType.DMA(shape)
    chips_n = cols_n // 2
    vmem = pl.BlockSpec(memory_space=pltpu.VMEM)
    hbm = pl.BlockSpec(memory_space=pl.ANY)
    smem = pl.BlockSpec(memory_space=pltpu.SMEM)
    own = jax.ShapeDtypeStruct((blocks, tile, width), bf16)
    split = lambda v: v.reshape(blocks, tile, width)
    hidden, grad_src, grad_dst, grads = pl.pallas_call(
        functools.partial(sage_kernel, sizes, scaling),
        out_shape=(own, own, own, jax.ShapeDtypeStruct((cols_n * piece, width), f32)),
        in_specs=[smem, hbm, hbm, vmem, vmem, vmem, hbm, hbm],
        out_specs=(vmem, vmem, vmem, vmem),
        scratch_shapes=[
            cube(blocks), cube(blocks), pltpu.VMEM((slots, tile, tile), bf16),
            cube(col_blocks), pltpu.VMEM((slots + 1, tile, width), f32),
            cube(row_blocks), cube(row_blocks), cube(row_blocks), cube(row_blocks),
            pltpu.VMEM((cols_n * piece, width), f32),
            cube(col_blocks), cube(chips_n * blocks), cube(chips_n * blocks),
            pltpu.VMEM((2 * width + 16, width), f32),
            pltpu.VMEM((cols_n * piece, width), bf16),
            pltpu.VMEM((cols_n - 1, piece, width), bf16),
            pltpu.VMEM((rows_n, piece, width), bf16),
            dma(4), dma(chips_n, chunks), dma(cols_n, chunks), dma(chips_n, chunks),
            dma(rows_n, chunks), dma(rows_n, chunks), dma(rows_n, chunks),
            dma(2, chunks), dma(rows_n, chunks), dma(rows_n, chunks),
            dma(chips_n, chunks), dma(chips_n, chunks), dma(chips_n, chunks), dma(chips_n, chunks),
            dma(cols_n - 1), dma(cols_n - 1), dma(rows_n - 1), dma(rows_n - 1), dma(cols_n - 1), dma(cols_n - 1),
        ],
        compiler_params=pltpu.CompilerParams(
            collective_id=0, has_side_effects=True, vmem_limit_bytes=50 * 2**20
        ),
        name="sage",
    )(idx, split(src_feats), split(dst_feats), w_self, w_neigh, bias[None, :], split(cotangent), cell_vals)
    flat = lambda v: v.reshape(own_rows, width)
    return (
        flat(hidden), flat(grad_src), flat(grad_dst),
        grads[:width], grads[width : 2 * width], grads[2 * width],
    )


def fits(own_rows, width, slots, tile):
    rows_n, cols_n = lax.axis_size("row"), lax.axis_size("col")
    block = own_rows * width * 2
    planned = block * (4 * rows_n + 3 * cols_n + 5) + slots * tile * (tile * 2 + width * 4)
    even = cols_n % 2 == 0 and rows_n > 1 and cols_n > 2
    return even and own_rows % (tile * CHUNKS) == 0 and planned < 40 * 2**20


def chosen(*args):
    slots, tile = args[6].shape[2:4]
    body = fused if fits(*args[0].shape, slots, tile) else local
    return body(*args)


def solution(mesh):
    return jax.shard_map(
        chosen,
        mesh=mesh,
        in_specs=(
            P(("groups", "row", "col"), None),
            P(("groups", "col", "row"), None),
            P(),
            P(),
            P(),
            P(("groups", "col", "row"), None),
            P(("groups", "col"), "row", None, None, None),
            P(("groups", "col"), "row", None),
            P(("groups", "col"), "row", None),
            P(("groups", "col"), "row"),
        ),
        out_specs=(
            P(("groups", "col", "row"), None),
            P(("groups", "row", "col"), None),
            P(("groups", "col", "row"), None),
            P("groups", None),
            P("groups", None),
            P("groups"),
        ),
        check_vma=False,
    )
```

```python
import functools
import math

import jax
import jax.numpy as jnp
from jax import lax
from jax.experimental import pallas as pl
from jax.experimental.pallas import tpu as pltpu
from jax.sharding import PartitionSpec as P

MESH = pl.DeviceIdType.MESH
CHUNKS = 8
FINISH_LAG = 2
PASS_LAG = 1
HOLD = 2
UNROLL = 8


def accumulate(tile_vals, out_index, in_index, live_count, source, out_blocks, flipped):
    tile_size = tile_vals.shape[-1]
    feature_width = source.shape[1]
    slot_total = tile_vals.shape[0]
    blocks = source.reshape(-1, tile_size, feature_width)
    group_size = min(32, slot_total)
    einsum_form = "tji,tjf->tif" if flipped else "tij,tjf->tif"

    def add_group(group_number, totals):
        first = group_number * group_size
        part_vals = lax.dynamic_slice_in_dim(tile_vals, first, group_size, 0)
        part_in = lax.dynamic_slice_in_dim(in_index, first, group_size, 0)
        part_out = lax.dynamic_slice_in_dim(out_index, first, group_size, 0)
        live = first + jnp.arange(group_size, dtype=jnp.int32) < live_count
        part_vals = jnp.where(live[:, None, None], part_vals, jnp.zeros((), part_vals.dtype))
        gathered = jnp.take(blocks, part_in, axis=0)
        product = jnp.einsum(einsum_form, part_vals, gathered, preferred_element_type=jnp.float32)
        return totals.at[part_out].add(product)

    initial = jnp.zeros((out_blocks, tile_size, feature_width), jnp.float32)
    turn_count = slot_total // group_size
    totals = lax.fori_loop(0, turn_count, add_group, initial)
    return totals.reshape(out_blocks * tile_size, feature_width)


def rounded_term(values):
    narrow = lax.optimization_barrier(values.astype(jnp.bfloat16))
    return narrow.astype(jnp.float32)


def dense_step(dst_rows, agg_rows, cot_rows, w_self, w_neigh, bias):
    preact = jnp.dot(dst_rows, w_self, preferred_element_type=jnp.float32)
    preact = preact + jnp.dot(agg_rows, w_neigh, preferred_element_type=jnp.float32) + bias
    gate_sig = jax.nn.sigmoid(preact)
    hidden_rows = (preact * gate_sig).astype(jnp.bfloat16)
    slope = gate_sig * (1.0 + preact * (1.0 - gate_sig))
    grad_rows = (cot_rows.astype(jnp.float32) * slope).astype(jnp.bfloat16)
    return (hidden_rows, grad_rows)


def local(
    src_feats,
    dst_feats,
    w_self,
    w_neigh,
    bias,
    cotangent,
    tile_vals,
    tile_rows,
    tile_cols,
    tile_count,
):
    cell_vals = tile_vals[0, 0]
    cell_rows = tile_rows[0, 0]
    cell_cols = tile_cols[0, 0]
    live_count = tile_count[0, 0]
    tile_size = cell_vals.shape[-1]
    own_rows = dst_feats.shape[0]
    row_blocks = own_rows * lax.axis_size("row") // tile_size
    col_blocks = src_feats.shape[0] * lax.axis_size("col") // tile_size
    source_block = lax.all_gather(src_feats, "col", axis=0, tiled=True)
    partial_value = rounded_term(
        accumulate(cell_vals, cell_rows, cell_cols, live_count, source_block, row_blocks, False)
    )
    aggregate = lax.psum_scatter(
        partial_value.astype(jnp.bfloat16), "row", scatter_dimension=0, tiled=True
    )
    hidden_out, grad_pre = dense_step(dst_feats, aggregate, cotangent, w_self, w_neigh, bias)
    back_own = jnp.dot(grad_pre, w_neigh.T, preferred_element_type=jnp.float32).astype(jnp.bfloat16)
    back_feats = lax.all_gather(back_own, "row", axis=0, tiled=True)
    grad_dst = jnp.dot(grad_pre, w_self.T, preferred_element_type=jnp.float32).astype(jnp.bfloat16)
    back_partial = rounded_term(
        accumulate(cell_vals, cell_cols, cell_rows, live_count, back_feats, col_blocks, True)
    )
    grad_src = lax.psum_scatter(
        back_partial.astype(jnp.bfloat16), "col", scatter_dimension=0, tiled=True
    )
    term_self = jnp.dot(dst_feats.T, grad_pre, preferred_element_type=jnp.float32)
    term_neigh = jnp.dot(aggregate.T, grad_pre, preferred_element_type=jnp.float32)
    term_bias = jnp.sum(grad_pre.astype(jnp.float32), axis=0)
    sum_self, sum_neigh, sum_bias = lax.psum((term_self, term_neigh, term_bias), ("row", "col"))
    scaling = 1.0 / math.sqrt(own_rows * lax.axis_size("row") * lax.axis_size("col"))
    return (
        hidden_out,
        grad_src,
        grad_dst,
        sum_self * scaling,
        sum_neigh * scaling,
        sum_bias * scaling,
    )


def sage_kernel(
    sizes, scaling, idx, src, dst_hbm, w_self, w_neigh, bias, cot_hbm, vals_hbm,
    hidden, grad_src, grad_dst, grads,
    dst, cot, vals, gathered, sums, part, from_low, from_high, back, grads_in,
    back_part, pair_in, chip_in, term_acc, terms, terms_in, terms_row,
    load_sem, src_send, src_recv, fwd_send, red_send, up_recv, down_recv,
    own_send, pass_send, back_recv, pair_send, pair_recv, chip_send, chip_recv,
    t1_send, t1_recv, t2_send, t2_recv, t3_send, t3_recv,
):
    rows_n, cols_n, slots, blocks, chunks, piece = sizes
    chips_n = cols_n // 2
    per = blocks // chunks
    tile = src.shape[1]
    width = src.shape[2]
    row_blocks = rows_n * blocks
    col_blocks = cols_n * blocks
    z = lax.axis_index("row")
    c = lax.axis_index("col")
    chip = c // 2
    core = c % 2
    sibling = chip * 2 + (1 - core)
    f32, bf16 = jnp.float32, jnp.bfloat16

    def remote(src_ref, dst_ref, send, recv, device):
        return pltpu.make_async_remote_copy(
            src_ref=src_ref, dst_ref=dst_ref, send_sem=send, recv_sem=recv,
            device_id=device, device_id_type=MESH,
        )

    loads = [
        pltpu.make_async_copy(src, gathered.at[pl.ds(c * blocks, blocks)], load_sem.at[0]),
        pltpu.make_async_copy(vals_hbm, vals, load_sem.at[1]),
        pltpu.make_async_copy(dst_hbm, dst, load_sem.at[2]),
        pltpu.make_async_copy(cot_hbm, cot, load_sem.at[3]),
    ]
    for load in loads:
        load.start()

    barrier = pltpu.get_barrier_semaphore()
    for k in range(1, cols_n):
        pl.semaphore_signal(barrier, inc=1, device_id={"col": lax.rem(c + k, cols_n)}, device_id_type=MESH)
    for k in range(1, rows_n):
        pl.semaphore_signal(barrier, inc=1, device_id={"row": lax.rem(z + k, rows_n)}, device_id_type=MESH)
    pl.semaphore_wait(barrier, cols_n + rows_n - 2)

    def src_copy(owner, k, sem_at, device, first):
        at = pl.ds(owner * blocks + k * per, per)
        from_ref = src.at[pl.ds(k * per, per)] if first else gathered.at[at]
        return remote(from_ref, gathered.at[at], src_send.at[sem_at, k], src_recv.at[owner, k], {"col": device})

    def far(dy):
        return lax.rem(chip + dy, chips_n) * 2 + core

    for k in range(chunks):
        for dy in range(1, chips_n):
            src_copy(c, k, dy, far(dy), True).start()
    for k in range(chunks):
        src_copy(c, k, 0, sibling, True).start()

    def src_pass(dy, k):
        owner = far(dy)
        at = pl.ds(owner * blocks + k * per, per)
        return remote(gathered.at[at], gathered.at[at], fwd_send.at[dy, k], src_recv.at[owner, k], {"col": sibling})

    sums[slots] = jnp.zeros((tile, width), f32)
    term_acc[...] = jnp.zeros_like(term_acc)

    for k in range(chunks):
        for dy in range(1, chips_n):
            src_copy(far(dy), k, dy, sibling, False).wait_recv()
            src_pass(dy, k).start()
    for load in loads[:2]:
        load.wait()
    for k in range(chunks):
        for y in range(chips_n):
            src_copy(y * 2 + 1 - core, k, 0, sibling, False).wait_recv()

    def forward_slot(s, carry):
        product = jnp.dot(vals[s], gathered[idx[1, s]], preferred_element_type=f32)
        sums[s] = product + sums[idx[2, s]]
        return carry

    lax.fori_loop(0, slots, forward_slot, 0, unroll=UNROLL)

    def forward_row(i, carry):
        part[i] = sums[idx[4, i]].astype(bf16)
        return carry

    lax.fori_loop(0, row_blocks, forward_row, 0, unroll=UNROLL)

    def at_of(d, k):
        return pl.ds(d * blocks + k * per, per)

    def up_copy(d, k, device):
        return remote(part.at[at_of(d, k)], from_low.at[at_of(d, k)], red_send.at[d, k], up_recv.at[d, k], {"row": device})

    def down_copy(d, k, device):
        return remote(part.at[at_of(d, k)], from_high.at[at_of(d, k)], red_send.at[d, k], down_recv.at[d, k], {"row": device})

    next_up = lax.rem(z + 1, rows_n)
    next_down = lax.rem(z + rows_n - 1, rows_n)

    def add_in(d, k, buf):
        at = at_of(d, k)
        part[at] = (part[at].astype(f32) + buf[at].astype(f32)).astype(bf16)

    def send_up(k):
        def step(i, carry):
            d = rows_n - 1 - i

            @pl.when(z > 0)
            def _():
                up_copy(d, k, next_up).wait_recv()
                add_in(d, k, from_low)

            @pl.when(k >= HOLD)
            def _():
                up_copy(d, k - HOLD, next_up).wait_send()

            up_copy(d, k, next_up).start()
            return carry

        lax.fori_loop(0, rows_n - 1 - z, step, 0)

    def send_down(k):
        def step(d, carry):
            @pl.when(z < rows_n - 1)
            def _():
                down_copy(d, k, next_down).wait_recv()
                add_in(d, k, from_high)

            @pl.when(k >= HOLD)
            def _():
                down_copy(d, k - HOLD, next_down).wait_send()

            down_copy(d, k, next_down).start()
            return carry

        lax.fori_loop(0, z, step, 0)

    is_end = jnp.logical_or(z == 0, z == rows_n - 1)
    is_low = z < rows_n // 2

    def stage_a(k):
        @pl.when(is_low)
        def _():
            send_up(k)

        @pl.when(jnp.logical_not(is_low))
        def _():
            send_down(k)

    def stage_b(k):
        @pl.when(is_low)
        def _():
            send_down(k)

        @pl.when(jnp.logical_not(is_low))
        def _():
            send_up(k)

    for load in loads[2:]:
        load.wait()

    def own_copy(k, way, device):
        at = at_of(z, k)
        return remote(back.at[at], back.at[at], own_send.at[way, k], back_recv.at[z, k], {"row": device})

    def pass_copy(owner, k, device):
        at = at_of(owner, k)
        return remote(back.at[at], back.at[at], pass_send.at[owner, k], back_recv.at[owner, k], {"row": device})

    def finish(k):
        @pl.when(z > 0)
        def _():
            up_copy(z, k, next_up).wait_recv()
            add_in(z, k, from_low)

        @pl.when(z < rows_n - 1)
        def _():
            down_copy(z, k, next_down).wait_recv()
            add_in(z, k, from_high)

        at = pl.ds(k * per, per)
        flat = (per * tile, width)
        agg_rows = part[at_of(z, k)].reshape(flat)
        dst_rows = dst[at].reshape(flat)
        preact = jnp.dot(dst_rows, w_self[...], preferred_element_type=f32)
        preact = preact + jnp.dot(agg_rows, w_neigh[...], preferred_element_type=f32) + bias[...]
        gate_sig = jax.nn.sigmoid(preact)
        slope = gate_sig * (1.0 + preact * (1.0 - gate_sig))
        grad_rows = (cot[at].reshape(flat).astype(f32) * slope).astype(bf16)
        turned = (((1,), (1,)), ((), ()))
        back_rows = lax.dot_general(grad_rows, w_neigh[...], turned, preferred_element_type=f32)
        back[at_of(z, k)] = back_rows.astype(bf16).reshape((per, tile, width))

        @pl.when(z < rows_n - 1)
        def _():
            own_copy(k, 0, next_up).start()

        @pl.when(z > 0)
        def _():
            own_copy(k, 1, next_down).start()

        hidden[at] = (preact * gate_sig).astype(bf16).reshape((per, tile, width))
        dst_grad = lax.dot_general(grad_rows, w_self[...], turned, preferred_element_type=f32)
        grad_dst[at] = dst_grad.astype(bf16).reshape((per, tile, width))
        outer = (((0,), (0,)), ((), ()))
        term_acc[pl.ds(0, width)] += lax.dot_general(dst_rows, grad_rows, outer, preferred_element_type=f32)
        term_acc[pl.ds(width, width)] += lax.dot_general(agg_rows, grad_rows, outer, preferred_element_type=f32)
        term_acc[pl.ds(2 * width, 8)] += jnp.sum(grad_rows.astype(f32).reshape((per * tile // 8, 8, width)), axis=0)

    def pass_on(j, k):
        @pl.when(jnp.logical_and(z >= j, z < rows_n - 1))
        def _():
            copy = pass_copy(z - j, k, next_up)
            copy.wait_recv()
            copy.start()

        @pl.when(jnp.logical_and(z + j < rows_n, z > 0))
        def _():
            copy = pass_copy(z + j, k, next_down)
            copy.wait_recv()
            copy.start()

    def turn(t, carry):
        @pl.when(jnp.logical_and(t < chunks, is_end))
        def _():
            stage_a(t)

        @pl.when(jnp.logical_and(t >= FINISH_LAG, t < chunks + FINISH_LAG))
        def _():
            finish(t - FINISH_LAG)

        for j in reversed(range(1, rows_n - 1)):
            lag = FINISH_LAG + j * PASS_LAG

            @pl.when(jnp.logical_and(t >= lag, t < chunks + lag))
            def _():
                pass_on(j, t - lag)

        @pl.when(jnp.logical_and(t >= 1, t < chunks + 1))
        def _():
            stage_b(t - 1)

        @pl.when(jnp.logical_and(t < chunks, jnp.logical_not(is_end)))
        def _():
            stage_a(t)

        return carry

    lax.fori_loop(0, chunks + FINISH_LAG, turn, 0)

    bias_sum = jnp.sum(term_acc[pl.ds(2 * width, 8)], axis=0, keepdims=True)
    spot = lax.broadcasted_iota(jnp.int32, (16, width), 0) == 0
    terms[pl.ds(0, 2 * width)] = term_acc[...][: 2 * width].astype(bf16)
    terms[pl.ds(2 * width, 16)] = jnp.where(spot, bias_sum, 0.0).astype(bf16)
    if cols_n * piece > 2 * width + 16:
        rest = cols_n * piece - 2 * width - 16
        terms[pl.ds(2 * width + 16, rest)] = jnp.zeros((rest, width), bf16)

    def t1_copy(k):
        peer = lax.rem(c + k, cols_n)
        return remote(terms.at[pl.ds(peer * piece, piece)], terms_in.at[k - 1], t1_send.at[k - 1], t1_recv.at[k - 1], {"col": peer})

    def t2_copy(k):
        peer = lax.rem(z + k, rows_n)
        return remote(terms_row.at[z], terms_row.at[z], t2_send.at[k - 1], t2_recv.at[k - 1], {"row": peer})

    def t3_copy(k):
        peer = lax.rem(c + k, cols_n)
        at = pl.ds(c * piece, piece)
        return remote(grads_in.at[at], grads_in.at[at], t3_send.at[k - 1], t3_recv.at[k - 1], {"col": peer})

    for k in range(1, cols_n):
        t1_copy(k).start()

    lax.fori_loop(chunks + FINISH_LAG, chunks + FINISH_LAG + (rows_n - 2) * PASS_LAG, turn, 0)

    total = terms[pl.ds(c * piece, piece)].astype(f32)
    for k in range(1, cols_n):
        t1_copy(k).wait_recv()
        total = total + terms_in[k - 1].astype(f32)
    terms_row[z] = total.astype(bf16)
    for k in range(1, rows_n):
        t2_copy(k).start()

    @pl.when(z == rows_n - 1)
    def _():
        for owner in range(rows_n - 1):
            for k in range(chunks):
                pass_copy(owner, k, next_down).wait_recv()

    @pl.when(z == 0)
    def _():
        for owner in range(1, rows_n):
            for k in range(chunks):
                pass_copy(owner, k, next_up).wait_recv()

    for k in range(1, rows_n):
        t2_copy(k).wait_recv()
    whole = terms_row[0].astype(f32)
    for k in range(1, rows_n):
        whole = whole + terms_row[k].astype(f32)
    grads_in[pl.ds(c * piece, piece)] = whole * scaling
    for k in range(1, cols_n):
        t3_copy(k).start()

    def backward_slot(s, carry):
        product = lax.dot_general(vals[s], back[idx[0, s]], (((0,), (0,)), ((), ())), preferred_element_type=f32)
        sums[s] = product + sums[idx[3, s]]
        return carry

    lax.fori_loop(0, slots, backward_slot, 0, unroll=UNROLL)

    def backward_block(owner):
        def each(i, carry):
            at = owner * blocks + i
            back_part[at] = sums[idx[5, at]].astype(bf16)
            return carry

        lax.fori_loop(0, blocks, each, 0, unroll=UNROLL)

    def pair_copy(dy, k):
        y = lax.rem(chip + dy, chips_n)
        owner = y * 2 + 1 - core
        return remote(
            back_part.at[at_of(owner, k)], pair_in.at[at_of(dy, k)],
            pair_send.at[dy, k], pair_recv.at[dy, k], {"col": sibling},
        )

    def chip_copy(dy, k):
        return remote(
            back_part.at[at_of(far(dy), k)], chip_in.at[at_of(dy, k)],
            chip_send.at[dy, k], chip_recv.at[dy, k], {"col": far(dy)},
        )

    order = list(range(1, chips_n)) + [0]
    for dy in order:
        backward_block(lax.rem(chip + dy, chips_n) * 2 + 1 - core)
        for k in range(chunks):
            pair_copy(dy, k).start()
        backward_block(far(dy))
    for dy in order:
        for k in range(chunks):
            pair_copy(dy, k).wait_recv()
            at = at_of(far(dy), k)
            back_part[at] = (back_part[at].astype(f32) + pair_in[at_of(dy, k)].astype(f32)).astype(bf16)
            if dy:
                chip_copy(dy, k).start()
    for k in range(chunks):
        summed = back_part[at_of(c, k)].astype(f32)
        for dy in range(1, chips_n):
            chip_copy(dy, k).wait_recv()
            summed = summed + chip_in[at_of(dy, k)].astype(f32)
        grad_src[pl.ds(k * per, per)] = summed.astype(bf16)

    for k in range(1, cols_n):
        t3_copy(k).wait_recv()
    grads[...] = grads_in[...]

    for k in range(chunks):
        src_copy(c, k, 0, sibling, True).wait_send()
        for dy in range(1, chips_n):
            src_copy(c, k, dy, far(dy), True).wait_send()
            src_pass(dy, k).wait_send()
            chip_copy(dy, k).wait_send()
        for dy in range(chips_n):
            pair_copy(dy, k).wait_send()
        for d in range(rows_n if k >= chunks - HOLD else 0):
            @pl.when(z != d)
            def _():
                up_copy(d, k, next_up).wait_send()

        @pl.when(z < rows_n - 1)
        def _():
            own_copy(k, 0, next_up).wait_send()

        @pl.when(z > 0)
        def _():
            own_copy(k, 1, next_down).wait_send()

        for d in range(rows_n):
            @pl.when(jnp.logical_and(z != d, jnp.logical_not(is_end)))
            def _():
                pass_copy(d, k, next_up).wait_send()
    for k in range(1, cols_n):
        t1_copy(k).wait_send()
        t3_copy(k).wait_send()
    for k in range(1, rows_n):
        t2_copy(k).wait_send()


def slot_links(keys, live, blocks):
    slots = keys.shape[0]
    place = jnp.arange(slots, dtype=jnp.int32)
    same = (keys[:, None] == keys[None, :]) & live[None, :] & (place[None, :] < place[:, None])
    before = jnp.max(jnp.where(same, place[None, :], -1), axis=1)
    hit = (jnp.arange(blocks, dtype=jnp.int32)[:, None] == keys[None, :]) & live[None, :]
    last = jnp.max(jnp.where(hit, place[None, :], -1), axis=1)
    return jnp.where(before < 0, slots, before), jnp.where(last < 0, slots, last)


def fused(src_feats, dst_feats, w_self, w_neigh, bias, cotangent, tile_vals, tile_rows, tile_cols, tile_count):
    cell_vals, cell_rows, cell_cols = tile_vals[0, 0], tile_rows[0, 0], tile_cols[0, 0]
    slots, tile = cell_vals.shape[:2]
    own_rows, width = src_feats.shape
    rows_n, cols_n = lax.axis_size("row"), lax.axis_size("col")
    blocks = own_rows // tile
    chunks = CHUNKS
    row_blocks, col_blocks = rows_n * blocks, cols_n * blocks
    piece = -(-(2 * width + 16) // (16 * cols_n)) * 16
    live = jnp.arange(slots, dtype=jnp.int32) < tile_count[0, 0]
    row_prev, row_last = slot_links(cell_rows, live, row_blocks)
    col_prev, col_last = slot_links(cell_cols, live, col_blocks)
    most = max(slots, row_blocks, col_blocks)
    lists = (cell_rows, cell_cols, row_prev, col_prev, row_last, col_last)
    idx = jnp.stack([jnp.pad(v, (0, most - v.shape[0])) for v in lists])
    scaling = 1.0 / math.sqrt(own_rows * rows_n * cols_n)
    sizes = (rows_n, cols_n, slots, blocks, chunks, piece)
    bf16, f32 = jnp.bfloat16, jnp.float32
    cube = lambda n: pltpu.VMEM((n, tile, width), bf16)
    dma = lambda *shape: pltpu.SemaphoreType.DMA(shape)
    chips_n = cols_n // 2
    vmem = pl.BlockSpec(memory_space=pltpu.VMEM)
    hbm = pl.BlockSpec(memory_space=pl.ANY)
    smem = pl.BlockSpec(memory_space=pltpu.SMEM)
    own = jax.ShapeDtypeStruct((blocks, tile, width), bf16)
    split = lambda v: v.reshape(blocks, tile, width)
    hidden, grad_src, grad_dst, grads = pl.pallas_call(
        functools.partial(sage_kernel, sizes, scaling),
        out_shape=(own, own, own, jax.ShapeDtypeStruct((cols_n * piece, width), f32)),
        in_specs=[smem, hbm, hbm, vmem, vmem, vmem, hbm, hbm],
        out_specs=(vmem, vmem, vmem, vmem),
        scratch_shapes=[
            cube(blocks), cube(blocks), pltpu.VMEM((slots, tile, tile), bf16),
            cube(col_blocks), pltpu.VMEM((slots + 1, tile, width), f32),
            cube(row_blocks), cube(row_blocks), cube(row_blocks), cube(row_blocks),
            pltpu.VMEM((cols_n * piece, width), f32),
            cube(col_blocks), cube(chips_n * blocks), cube(chips_n * blocks),
            pltpu.VMEM((2 * width + 16, width), f32),
            pltpu.VMEM((cols_n * piece, width), bf16),
            pltpu.VMEM((cols_n - 1, piece, width), bf16),
            pltpu.VMEM((rows_n, piece, width), bf16),
            dma(4), dma(chips_n, chunks), dma(cols_n, chunks), dma(chips_n, chunks),
            dma(rows_n, chunks), dma(rows_n, chunks), dma(rows_n, chunks),
            dma(2, chunks), dma(rows_n, chunks), dma(rows_n, chunks),
            dma(chips_n, chunks), dma(chips_n, chunks), dma(chips_n, chunks), dma(chips_n, chunks),
            dma(cols_n - 1), dma(cols_n - 1), dma(rows_n - 1), dma(rows_n - 1), dma(cols_n - 1), dma(cols_n - 1),
        ],
        compiler_params=pltpu.CompilerParams(
            collective_id=0, has_side_effects=True, vmem_limit_bytes=61 * 2**20
        ),
        name="sage",
    )(idx, split(src_feats), split(dst_feats), w_self, w_neigh, bias[None, :], split(cotangent), cell_vals)
    flat = lambda v: v.reshape(own_rows, width)
    return (
        flat(hidden), flat(grad_src), flat(grad_dst),
        grads[:width], grads[width : 2 * width], grads[2 * width],
    )


def fits(own_rows, width, slots, tile):
    rows_n, cols_n = lax.axis_size("row"), lax.axis_size("col")
    block = own_rows * width * 2
    planned = block * (4 * rows_n + 3 * cols_n + 5) + slots * tile * (tile * 2 + width * 4)
    even = cols_n % 2 == 0 and rows_n > 1 and cols_n > 2
    return even and own_rows % (tile * CHUNKS) == 0 and planned < 40 * 2**20


def chosen(*args):
    slots, tile = args[6].shape[2:4]
    body = fused if fits(*args[0].shape, slots, tile) else local
    return body(*args)


def solution(mesh):
    return jax.shard_map(
        chosen,
        mesh=mesh,
        in_specs=(
            P(("groups", "row", "col"), None),
            P(("groups", "col", "row"), None),
            P(),
            P(),
            P(),
            P(("groups", "col", "row"), None),
            P(("groups", "col"), "row", None, None, None),
            P(("groups", "col"), "row", None),
            P(("groups", "col"), "row", None),
            P(("groups", "col"), "row"),
        ),
        out_specs=(
            P(("groups", "col", "row"), None),
            P(("groups", "row", "col"), None),
            P(("groups", "col", "row"), None),
            P("groups", None),
            P("groups", None),
            P("groups"),
        ),
        check_vma=False,
    )
```

```python
import functools
import math

import jax
import jax.numpy as jnp
from jax import lax
from jax.experimental import pallas as pl
from jax.experimental.pallas import tpu as pltpu
from jax.sharding import PartitionSpec as P

MESH = pl.DeviceIdType.MESH
CHUNKS = 8
FINISH_LAG = 2
PASS_LAG = 1
HOLD = 2
UNROLL = 8


def accumulate(tile_vals, out_index, in_index, live_count, source, out_blocks, flipped):
    tile_size = tile_vals.shape[-1]
    feature_width = source.shape[1]
    slot_total = tile_vals.shape[0]
    blocks = source.reshape(-1, tile_size, feature_width)
    group_size = min(32, slot_total)
    einsum_form = "tji,tjf->tif" if flipped else "tij,tjf->tif"

    def add_group(group_number, totals):
        first = group_number * group_size
        part_vals = lax.dynamic_slice_in_dim(tile_vals, first, group_size, 0)
        part_in = lax.dynamic_slice_in_dim(in_index, first, group_size, 0)
        part_out = lax.dynamic_slice_in_dim(out_index, first, group_size, 0)
        live = first + jnp.arange(group_size, dtype=jnp.int32) < live_count
        part_vals = jnp.where(live[:, None, None], part_vals, jnp.zeros((), part_vals.dtype))
        gathered = jnp.take(blocks, part_in, axis=0)
        product = jnp.einsum(einsum_form, part_vals, gathered, preferred_element_type=jnp.float32)
        return totals.at[part_out].add(product)

    initial = jnp.zeros((out_blocks, tile_size, feature_width), jnp.float32)
    turn_count = slot_total // group_size
    totals = lax.fori_loop(0, turn_count, add_group, initial)
    return totals.reshape(out_blocks * tile_size, feature_width)


def rounded_term(values):
    narrow = lax.optimization_barrier(values.astype(jnp.bfloat16))
    return narrow.astype(jnp.float32)


def dense_step(dst_rows, agg_rows, cot_rows, w_self, w_neigh, bias):
    preact = jnp.dot(dst_rows, w_self, preferred_element_type=jnp.float32)
    preact = preact + jnp.dot(agg_rows, w_neigh, preferred_element_type=jnp.float32) + bias
    gate_sig = jax.nn.sigmoid(preact)
    hidden_rows = (preact * gate_sig).astype(jnp.bfloat16)
    slope = gate_sig * (1.0 + preact * (1.0 - gate_sig))
    grad_rows = (cot_rows.astype(jnp.float32) * slope).astype(jnp.bfloat16)
    return (hidden_rows, grad_rows)


def local(
    src_feats,
    dst_feats,
    w_self,
    w_neigh,
    bias,
    cotangent,
    tile_vals,
    tile_rows,
    tile_cols,
    tile_count,
):
    cell_vals = tile_vals[0, 0]
    cell_rows = tile_rows[0, 0]
    cell_cols = tile_cols[0, 0]
    live_count = tile_count[0, 0]
    tile_size = cell_vals.shape[-1]
    own_rows = dst_feats.shape[0]
    row_blocks = own_rows * lax.axis_size("row") // tile_size
    col_blocks = src_feats.shape[0] * lax.axis_size("col") // tile_size
    source_block = lax.all_gather(src_feats, "col", axis=0, tiled=True)
    partial_value = rounded_term(
        accumulate(cell_vals, cell_rows, cell_cols, live_count, source_block, row_blocks, False)
    )
    aggregate = lax.psum_scatter(
        partial_value.astype(jnp.bfloat16), "row", scatter_dimension=0, tiled=True
    )
    hidden_out, grad_pre = dense_step(dst_feats, aggregate, cotangent, w_self, w_neigh, bias)
    back_own = jnp.dot(grad_pre, w_neigh.T, preferred_element_type=jnp.float32).astype(jnp.bfloat16)
    back_feats = lax.all_gather(back_own, "row", axis=0, tiled=True)
    grad_dst = jnp.dot(grad_pre, w_self.T, preferred_element_type=jnp.float32).astype(jnp.bfloat16)
    back_partial = rounded_term(
        accumulate(cell_vals, cell_cols, cell_rows, live_count, back_feats, col_blocks, True)
    )
    grad_src = lax.psum_scatter(
        back_partial.astype(jnp.bfloat16), "col", scatter_dimension=0, tiled=True
    )
    term_self = jnp.dot(dst_feats.T, grad_pre, preferred_element_type=jnp.float32)
    term_neigh = jnp.dot(aggregate.T, grad_pre, preferred_element_type=jnp.float32)
    term_bias = jnp.sum(grad_pre.astype(jnp.float32), axis=0)
    sum_self, sum_neigh, sum_bias = lax.psum((term_self, term_neigh, term_bias), ("row", "col"))
    scaling = 1.0 / math.sqrt(own_rows * lax.axis_size("row") * lax.axis_size("col"))
    return (
        hidden_out,
        grad_src,
        grad_dst,
        sum_self * scaling,
        sum_neigh * scaling,
        sum_bias * scaling,
    )


def sage_kernel(
    sizes, scaling, idx, src, dst_hbm, w_self, w_neigh, bias, cot_hbm, vals_hbm,
    hidden, grad_src, grad_dst, grads_self, grads_neigh, grads_bias,
    dst, cot, vals, gathered, sums, part, from_low, from_high, back, grads_in,
    back_part, pair_in, chip_in, term_acc, terms, terms_in, terms_row,
    load_sem, src_send, src_recv, fwd_send, red_send, up_recv, down_recv,
    own_send, pass_send, back_recv, pair_send, pair_recv, chip_send, chip_recv,
    t1_send, t1_recv, t2_send, t2_recv, t3_send, t3_recv,
):
    rows_n, cols_n, slots, blocks, chunks, piece = sizes
    chips_n = cols_n // 2
    per = blocks // chunks
    tile = src.shape[1]
    width = src.shape[2]
    row_blocks = rows_n * blocks
    col_blocks = cols_n * blocks
    z = lax.axis_index("row")
    c = lax.axis_index("col")
    chip = c // 2
    core = c % 2
    sibling = chip * 2 + (1 - core)
    f32, bf16 = jnp.float32, jnp.bfloat16

    def remote(src_ref, dst_ref, send, recv, device):
        return pltpu.make_async_remote_copy(
            src_ref=src_ref, dst_ref=dst_ref, send_sem=send, recv_sem=recv,
            device_id=device, device_id_type=MESH,
        )

    loads = [
        pltpu.make_async_copy(src, gathered.at[pl.ds(c * blocks, blocks)], load_sem.at[0]),
        pltpu.make_async_copy(vals_hbm, vals, load_sem.at[1]),
        pltpu.make_async_copy(dst_hbm, dst, load_sem.at[2]),
        pltpu.make_async_copy(cot_hbm, cot, load_sem.at[3]),
    ]
    for load in loads:
        load.start()

    barrier = pltpu.get_barrier_semaphore()
    for k in range(1, cols_n):
        pl.semaphore_signal(barrier, inc=1, device_id={"col": lax.rem(c + k, cols_n)}, device_id_type=MESH)
    for k in range(1, rows_n):
        pl.semaphore_signal(barrier, inc=1, device_id={"row": lax.rem(z + k, rows_n)}, device_id_type=MESH)
    pl.semaphore_wait(barrier, cols_n + rows_n - 2)

    def src_copy(owner, k, sem_at, device, first):
        at = pl.ds(owner * blocks + k * per, per)
        from_ref = src.at[pl.ds(k * per, per)] if first else gathered.at[at]
        return remote(from_ref, gathered.at[at], src_send.at[sem_at, k], src_recv.at[owner, k], {"col": device})

    def far(dy):
        return lax.rem(chip + dy, chips_n) * 2 + core

    for k in range(chunks):
        for dy in range(1, chips_n):
            src_copy(c, k, dy, far(dy), True).start()
    for k in range(chunks):
        src_copy(c, k, 0, sibling, True).start()

    def src_pass(dy, k):
        owner = far(dy)
        at = pl.ds(owner * blocks + k * per, per)
        return remote(gathered.at[at], gathered.at[at], fwd_send.at[dy, k], src_recv.at[owner, k], {"col": sibling})

    sums[slots] = jnp.zeros((tile, width), f32)
    term_acc[...] = jnp.zeros_like(term_acc)

    for k in range(chunks):
        for dy in range(1, chips_n):
            src_copy(far(dy), k, dy, sibling, False).wait_recv()
            src_pass(dy, k).start()
    for load in loads[:2]:
        load.wait()
    for k in range(chunks):
        for y in range(chips_n):
            src_copy(y * 2 + 1 - core, k, 0, sibling, False).wait_recv()

    def forward_slot(s, carry):
        product = jnp.dot(vals[s], gathered[idx[1, s]], preferred_element_type=f32)
        sums[s] = product + sums[idx[2, s]]
        return carry

    lax.fori_loop(0, slots, forward_slot, 0, unroll=UNROLL)

    def forward_row(i, carry):
        part[i] = sums[idx[4, i]].astype(bf16)
        return carry

    lax.fori_loop(0, row_blocks, forward_row, 0, unroll=UNROLL)

    def at_of(d, k):
        return pl.ds(d * blocks + k * per, per)

    def up_copy(d, k, device):
        return remote(part.at[at_of(d, k)], from_low.at[at_of(d, k)], red_send.at[d, k], up_recv.at[d, k], {"row": device})

    def down_copy(d, k, device):
        return remote(part.at[at_of(d, k)], from_high.at[at_of(d, k)], red_send.at[d, k], down_recv.at[d, k], {"row": device})

    next_up = lax.rem(z + 1, rows_n)
    next_down = lax.rem(z + rows_n - 1, rows_n)

    def add_in(d, k, buf):
        at = at_of(d, k)
        part[at] = (part[at].astype(f32) + buf[at].astype(f32)).astype(bf16)

    def send_up(k):
        def step(i, carry):
            d = rows_n - 1 - i

            @pl.when(z > 0)
            def _():
                up_copy(d, k, next_up).wait_recv()
                add_in(d, k, from_low)

            @pl.when(k >= HOLD)
            def _():
                up_copy(d, k - HOLD, next_up).wait_send()

            up_copy(d, k, next_up).start()
            return carry

        lax.fori_loop(0, rows_n - 1 - z, step, 0)

    def send_down(k):
        def step(d, carry):
            @pl.when(z < rows_n - 1)
            def _():
                down_copy(d, k, next_down).wait_recv()
                add_in(d, k, from_high)

            @pl.when(k >= HOLD)
            def _():
                down_copy(d, k - HOLD, next_down).wait_send()

            down_copy(d, k, next_down).start()
            return carry

        lax.fori_loop(0, z, step, 0)

    is_end = jnp.logical_or(z == 0, z == rows_n - 1)
    is_low = z < rows_n // 2

    def stage_a(k):
        @pl.when(is_low)
        def _():
            send_up(k)

        @pl.when(jnp.logical_not(is_low))
        def _():
            send_down(k)

    def stage_b(k):
        @pl.when(is_low)
        def _():
            send_down(k)

        @pl.when(jnp.logical_not(is_low))
        def _():
            send_up(k)

    for load in loads[2:]:
        load.wait()

    def own_copy(k, way, device):
        at = at_of(z, k)
        return remote(back.at[at], back.at[at], own_send.at[way, k], back_recv.at[z, k], {"row": device})

    def pass_copy(owner, k, device):
        at = at_of(owner, k)
        return remote(back.at[at], back.at[at], pass_send.at[owner, k], back_recv.at[owner, k], {"row": device})

    def finish(k):
        @pl.when(z > 0)
        def _():
            up_copy(z, k, next_up).wait_recv()
            add_in(z, k, from_low)

        @pl.when(z < rows_n - 1)
        def _():
            down_copy(z, k, next_down).wait_recv()
            add_in(z, k, from_high)

        at = pl.ds(k * per, per)
        flat = (per * tile, width)
        agg_rows = part[at_of(z, k)].reshape(flat)
        dst_rows = dst[at].reshape(flat)
        preact = jnp.dot(dst_rows, w_self[...], preferred_element_type=f32)
        preact = preact + jnp.dot(agg_rows, w_neigh[...], preferred_element_type=f32) + bias[...]
        gate_sig = jax.nn.sigmoid(preact)
        slope = gate_sig * (1.0 + preact * (1.0 - gate_sig))
        grad_rows = (cot[at].reshape(flat).astype(f32) * slope).astype(bf16)
        turned = (((1,), (1,)), ((), ()))
        back_rows = lax.dot_general(grad_rows, w_neigh[...], turned, preferred_element_type=f32)
        back[at_of(z, k)] = back_rows.astype(bf16).reshape((per, tile, width))

        @pl.when(z < rows_n - 1)
        def _():
            own_copy(k, 0, next_up).start()

        @pl.when(z > 0)
        def _():
            own_copy(k, 1, next_down).start()

        hidden[at] = (preact * gate_sig).astype(bf16).reshape((per, tile, width))
        dst_grad = lax.dot_general(grad_rows, w_self[...], turned, preferred_element_type=f32)
        grad_dst[at] = dst_grad.astype(bf16).reshape((per, tile, width))
        outer = (((0,), (0,)), ((), ()))
        term_acc[pl.ds(0, width)] += lax.dot_general(dst_rows, grad_rows, outer, preferred_element_type=f32)
        term_acc[pl.ds(width, width)] += lax.dot_general(agg_rows, grad_rows, outer, preferred_element_type=f32)
        term_acc[pl.ds(2 * width, 8)] += jnp.sum(grad_rows.astype(f32).reshape((per * tile // 8, 8, width)), axis=0)

    def pass_on(j, k):
        @pl.when(jnp.logical_and(z >= j, z < rows_n - 1))
        def _():
            copy = pass_copy(z - j, k, next_up)
            copy.wait_recv()
            copy.start()

        @pl.when(jnp.logical_and(z + j < rows_n, z > 0))
        def _():
            copy = pass_copy(z + j, k, next_down)
            copy.wait_recv()
            copy.start()

    def turn(t, carry):
        @pl.when(jnp.logical_and(t < chunks, is_end))
        def _():
            stage_a(t)

        @pl.when(jnp.logical_and(t >= FINISH_LAG, t < chunks + FINISH_LAG))
        def _():
            finish(t - FINISH_LAG)

        for j in reversed(range(1, rows_n - 1)):
            lag = FINISH_LAG + j * PASS_LAG

            @pl.when(jnp.logical_and(t >= lag, t < chunks + lag))
            def _():
                pass_on(j, t - lag)

        @pl.when(jnp.logical_and(t >= 1, t < chunks + 1))
        def _():
            stage_b(t - 1)

        @pl.when(jnp.logical_and(t < chunks, jnp.logical_not(is_end)))
        def _():
            stage_a(t)

        return carry

    lax.fori_loop(0, chunks + FINISH_LAG, turn, 0)

    bias_sum = jnp.sum(term_acc[pl.ds(2 * width, 8)], axis=0, keepdims=True)
    spot = lax.broadcasted_iota(jnp.int32, (16, width), 0) == 0
    terms[pl.ds(0, 2 * width)] = term_acc[...][: 2 * width].astype(bf16)
    terms[pl.ds(2 * width, 16)] = jnp.where(spot, bias_sum, 0.0).astype(bf16)
    if cols_n * piece > 2 * width + 16:
        rest = cols_n * piece - 2 * width - 16
        terms[pl.ds(2 * width + 16, rest)] = jnp.zeros((rest, width), bf16)

    def t1_copy(k):
        peer = lax.rem(c + k, cols_n)
        return remote(terms.at[pl.ds(peer * piece, piece)], terms_in.at[k - 1], t1_send.at[k - 1], t1_recv.at[k - 1], {"col": peer})

    def t2_copy(k):
        peer = lax.rem(z + k, rows_n)
        return remote(terms_row.at[z], terms_row.at[z], t2_send.at[k - 1], t2_recv.at[k - 1], {"row": peer})

    def t3_copy(k):
        peer = lax.rem(c + k, cols_n)
        at = pl.ds(c * piece, piece)
        return remote(grads_in.at[at], grads_in.at[at], t3_send.at[k - 1], t3_recv.at[k - 1], {"col": peer})

    for k in range(1, cols_n):
        t1_copy(k).start()

    lax.fori_loop(chunks + FINISH_LAG, chunks + FINISH_LAG + (rows_n - 2) * PASS_LAG, turn, 0)

    total = terms[pl.ds(c * piece, piece)].astype(f32)
    for k in range(1, cols_n):
        t1_copy(k).wait_recv()
        total = total + terms_in[k - 1].astype(f32)
    terms_row[z] = total.astype(bf16)
    for k in range(1, rows_n):
        t2_copy(k).start()

    @pl.when(z == rows_n - 1)
    def _():
        for owner in range(rows_n - 1):
            for k in range(chunks):
                pass_copy(owner, k, next_down).wait_recv()

    @pl.when(z == 0)
    def _():
        for owner in range(1, rows_n):
            for k in range(chunks):
                pass_copy(owner, k, next_up).wait_recv()

    for k in range(1, rows_n):
        t2_copy(k).wait_recv()
    whole = terms_row[0].astype(f32)
    for k in range(1, rows_n):
        whole = whole + terms_row[k].astype(f32)
    grads_in[pl.ds(c * piece, piece)] = whole * scaling
    for k in range(1, cols_n):
        t3_copy(k).start()

    def backward_slot(s, carry):
        product = lax.dot_general(vals[s], back[idx[0, s]], (((0,), (0,)), ((), ())), preferred_element_type=f32)
        sums[s] = product + sums[idx[3, s]]
        return carry

    lax.fori_loop(0, slots, backward_slot, 0, unroll=UNROLL)

    def backward_block(owner):
        def each(i, carry):
            at = owner * blocks + i
            back_part[at] = sums[idx[5, at]].astype(bf16)
            return carry

        lax.fori_loop(0, blocks, each, 0, unroll=UNROLL)

    def pair_copy(dy, k):
        y = lax.rem(chip + dy, chips_n)
        owner = y * 2 + 1 - core
        return remote(
            back_part.at[at_of(owner, k)], pair_in.at[at_of(dy, k)],
            pair_send.at[dy, k], pair_recv.at[dy, k], {"col": sibling},
        )

    def chip_copy(dy, k):
        return remote(
            back_part.at[at_of(far(dy), k)], chip_in.at[at_of(dy, k)],
            chip_send.at[dy, k], chip_recv.at[dy, k], {"col": far(dy)},
        )

    order = list(range(1, chips_n)) + [0]
    for dy in order:
        backward_block(lax.rem(chip + dy, chips_n) * 2 + 1 - core)
        for k in range(chunks):
            pair_copy(dy, k).start()
        backward_block(far(dy))
    for dy in order:
        for k in range(chunks):
            pair_copy(dy, k).wait_recv()
            at = at_of(far(dy), k)
            back_part[at] = (back_part[at].astype(f32) + pair_in[at_of(dy, k)].astype(f32)).astype(bf16)
            if dy:
                chip_copy(dy, k).start()
    for k in range(chunks):
        summed = back_part[at_of(c, k)].astype(f32)
        for dy in range(1, chips_n):
            chip_copy(dy, k).wait_recv()
            summed = summed + chip_in[at_of(dy, k)].astype(f32)
        grad_src[pl.ds(k * per, per)] = summed.astype(bf16)

    for k in range(1, cols_n):
        t3_copy(k).wait_recv()
    grads_self[...] = grads_in[pl.ds(0, width)]
    grads_neigh[...] = grads_in[pl.ds(width, width)]
    grads_bias[...] = grads_in[pl.ds(2 * width, 8)]

    for k in range(chunks):
        src_copy(c, k, 0, sibling, True).wait_send()
        for dy in range(1, chips_n):
            src_copy(c, k, dy, far(dy), True).wait_send()
            src_pass(dy, k).wait_send()
            chip_copy(dy, k).wait_send()
        for dy in range(chips_n):
            pair_copy(dy, k).wait_send()
        for d in range(rows_n if k >= chunks - HOLD else 0):
            @pl.when(z != d)
            def _():
                up_copy(d, k, next_up).wait_send()

        @pl.when(z < rows_n - 1)
        def _():
            own_copy(k, 0, next_up).wait_send()

        @pl.when(z > 0)
        def _():
            own_copy(k, 1, next_down).wait_send()

        for d in range(rows_n):
            @pl.when(jnp.logical_and(z != d, jnp.logical_not(is_end)))
            def _():
                pass_copy(d, k, next_up).wait_send()
    for k in range(1, cols_n):
        t1_copy(k).wait_send()
        t3_copy(k).wait_send()
    for k in range(1, rows_n):
        t2_copy(k).wait_send()


def slot_links(keys, live, blocks):
    slots = keys.shape[0]
    place = jnp.arange(slots, dtype=jnp.int32)
    same = (keys[:, None] == keys[None, :]) & live[None, :] & (place[None, :] < place[:, None])
    before = jnp.max(jnp.where(same, place[None, :], -1), axis=1)
    hit = (jnp.arange(blocks, dtype=jnp.int32)[:, None] == keys[None, :]) & live[None, :]
    last = jnp.max(jnp.where(hit, place[None, :], -1), axis=1)
    return jnp.where(before < 0, slots, before), jnp.where(last < 0, slots, last)


def fused(src_feats, dst_feats, w_self, w_neigh, bias, cotangent, tile_vals, tile_rows, tile_cols, tile_count):
    cell_vals, cell_rows, cell_cols = tile_vals[0, 0], tile_rows[0, 0], tile_cols[0, 0]
    slots, tile = cell_vals.shape[:2]
    own_rows, width = src_feats.shape
    rows_n, cols_n = lax.axis_size("row"), lax.axis_size("col")
    blocks = own_rows // tile
    chunks = CHUNKS
    row_blocks, col_blocks = rows_n * blocks, cols_n * blocks
    piece = -(-(2 * width + 16) // (16 * cols_n)) * 16
    live = jnp.arange(slots, dtype=jnp.int32) < tile_count[0, 0]
    row_prev, row_last = slot_links(cell_rows, live, row_blocks)
    col_prev, col_last = slot_links(cell_cols, live, col_blocks)
    most = max(slots, row_blocks, col_blocks)
    lists = (cell_rows, cell_cols, row_prev, col_prev, row_last, col_last)
    idx = jnp.stack([jnp.pad(v, (0, most - v.shape[0])) for v in lists])
    scaling = 1.0 / math.sqrt(own_rows * rows_n * cols_n)
    sizes = (rows_n, cols_n, slots, blocks, chunks, piece)
    bf16, f32 = jnp.bfloat16, jnp.float32
    cube = lambda n: pltpu.VMEM((n, tile, width), bf16)
    dma = lambda *shape: pltpu.SemaphoreType.DMA(shape)
    chips_n = cols_n // 2
    vmem = pl.BlockSpec(memory_space=pltpu.VMEM)
    hbm = pl.BlockSpec(memory_space=pl.ANY)
    smem = pl.BlockSpec(memory_space=pltpu.SMEM)
    own = jax.ShapeDtypeStruct((blocks, tile, width), bf16)
    term = jax.ShapeDtypeStruct((width, width), f32)
    split = lambda v: v.reshape(blocks, tile, width)
    hidden, grad_src, grad_dst, grads_self, grads_neigh, grads_bias = pl.pallas_call(
        functools.partial(sage_kernel, sizes, scaling),
        out_shape=(own, own, own, term, term, jax.ShapeDtypeStruct((8, width), f32)),
        in_specs=[smem, hbm, hbm, vmem, vmem, vmem, hbm, hbm],
        out_specs=(vmem,) * 6,
        scratch_shapes=[
            cube(blocks), cube(blocks), pltpu.VMEM((slots, tile, tile), bf16),
            cube(col_blocks), pltpu.VMEM((slots + 1, tile, width), f32),
            cube(row_blocks), cube(row_blocks), cube(row_blocks), cube(row_blocks),
            pltpu.VMEM((cols_n * piece, width), f32),
            cube(col_blocks), cube(chips_n * blocks), cube(chips_n * blocks),
            pltpu.VMEM((2 * width + 16, width), f32),
            pltpu.VMEM((cols_n * piece, width), bf16),
            pltpu.VMEM((cols_n - 1, piece, width), bf16),
            pltpu.VMEM((rows_n, piece, width), bf16),
            dma(4), dma(chips_n, chunks), dma(cols_n, chunks), dma(chips_n, chunks),
            dma(rows_n, chunks), dma(rows_n, chunks), dma(rows_n, chunks),
            dma(2, chunks), dma(rows_n, chunks), dma(rows_n, chunks),
            dma(chips_n, chunks), dma(chips_n, chunks), dma(chips_n, chunks), dma(chips_n, chunks),
            dma(cols_n - 1), dma(cols_n - 1), dma(rows_n - 1), dma(rows_n - 1), dma(cols_n - 1), dma(cols_n - 1),
        ],
        compiler_params=pltpu.CompilerParams(
            collective_id=0, has_side_effects=True, vmem_limit_bytes=61 * 2**20
        ),
        name="sage",
    )(idx, split(src_feats), split(dst_feats), w_self, w_neigh, bias[None, :], split(cotangent), cell_vals)
    flat = lambda v: v.reshape(own_rows, width)
    return (
        flat(hidden), flat(grad_src), flat(grad_dst),
        grads_self, grads_neigh, grads_bias[0],
    )


def fits(own_rows, width, slots, tile):
    rows_n, cols_n = lax.axis_size("row"), lax.axis_size("col")
    block = own_rows * width * 2
    planned = block * (4 * rows_n + 3 * cols_n + 5) + slots * tile * (tile * 2 + width * 4)
    even = cols_n % 2 == 0 and rows_n > 1 and cols_n > 2
    return even and own_rows % (tile * CHUNKS) == 0 and planned < 40 * 2**20


def chosen(*args):
    slots, tile = args[6].shape[2:4]
    body = fused if fits(*args[0].shape, slots, tile) else local
    return body(*args)


def solution(mesh):
    return jax.shard_map(
        chosen,
        mesh=mesh,
        in_specs=(
            P(("groups", "row", "col"), None),
            P(("groups", "col", "row"), None),
            P(),
            P(),
            P(),
            P(("groups", "col", "row"), None),
            P(("groups", "col"), "row", None, None, None),
            P(("groups", "col"), "row", None),
            P(("groups", "col"), "row", None),
            P(("groups", "col"), "row"),
        ),
        out_specs=(
            P(("groups", "col", "row"), None),
            P(("groups", "row", "col"), None),
            P(("groups", "col", "row"), None),
            P("groups", None),
            P("groups", None),
            P("groups"),
        ),
        check_vma=False,
    )
```
